256 devices in a mesh: prow: 16 (over z, core), pcol: 16 (over y, x).
Axes of the slice: x: 4, y: 4, z: 8, core: 2. Of those that a mesh axis runs over, the one named last changes fastest.
Arguments:
- factor_blocks: bfloat16 [7, 2048, 256, 256], P(None, ('prow', 'pcol')), may hold values from -0.125 to 0.125
- block_column: int32 [7, 2048], P(None, ('prow', 'pcol')), may hold values from 0 to 15
- block_row: int32 [7, 2048], P(None, ('prow', 'pcol')), may hold values from 16 to 127, as said below
- block_count: int32 [7, 256], P(None, ('prow', 'pcol')), may hold values from 1 to 8, as said below
- diag_inverse: bfloat16 [8, 256, 256, 256], P(None, ('prow', 'pcol')), as said below
- right_side: float32 [8, 256, 64, 256], P(None, ('prow', 'pcol')), may hold values from -6 to 6
Outputs:
- forward_solution: float32 [8, 256, 64, 256], P(None, ('prow', 'pcol'))
- solution: float32 [8, 256, 64, 256], P(None, ('prow', 'pcol'))
The draws below stay inside these ranges and needn't reach their ends.
Inputs may be any that keep to these rules, and one draw needn't show every extreme that they name: Every slot of level l, live or not, names a row supernode of a later level: block_row[l, s] >= (l + 1) * 16. `block_count`: at every level some device has all 8 slots live. `diag_inverse`: each matrix is the identity plus an off-diagonal part.
All inputs are finite; a program needn't handle non-finite values.
Results may differ from the reference program's by a relative error of at most 0.015.
Values may be sent and summed in bfloat16 or wider, within the bound.
A program may use at most 128 MiB of HBM per device.

```python
import jax
import jax.numpy as jnp
from jax import lax

B = 256
R = 64
LEVELS = 8
BLK = 8
GRID_ROWS = 16
GRID_COLS = 16
NODES = 256
SLOTS = 2048


def draw_block_row(key, part):
    key = jax.random.fold_in(key, 11)
    lowest = ((jnp.arange(LEVELS - 1, dtype=jnp.int32) + 1) * GRID_COLS)[:, None]
    return jax.random.randint(key, (LEVELS - 1, SLOTS), lowest, LEVELS * GRID_COLS, dtype=jnp.int32)


def draw_block_count(key, part):
    key = jax.random.fold_in(key, 23)
    first_key, second_key = jax.random.split(key)
    counts = jax.random.randint(first_key, (LEVELS - 1, NODES), 1, BLK + 1, dtype=jnp.int32)
    busiest = jax.random.randint(second_key, (LEVELS - 1, 1), 0, NODES, dtype=jnp.int32)
    column_ids = jnp.arange(NODES, dtype=jnp.int32)[None, :]
    return jnp.where(column_ids == busiest, BLK, counts).astype(jnp.int32)


def draw_diag_inverse(key, part):
    key = jax.random.fold_in(key, 37)
    shape = (LEVELS, NODES, B, B)
    spread = 0.4 / B ** 0.5
    noise = jax.random.normal(key, shape, jnp.float32) * spread
    eye = (jnp.arange(B)[:, None] == jnp.arange(B)[None, :]).astype(jnp.float32)
    return (eye + noise * (1.0 - eye)).astype(jnp.bfloat16)


def place_ends(values, rng, low, largest):
    spot = [jax.random.randint(jax.random.fold_in(rng, axis), (), 0, length) for axis, length in enumerate(values.shape)]
    main_axis = values.shape.index(max(values.shape))
    next_to = spot[:main_axis] + [(spot[main_axis] + 1) % values.shape[main_axis]] + spot[main_axis + 1:]
    return values.at[tuple(spot)].set(low).at[tuple(next_to)].set(largest)


def shard_levels(rng, dims, pieces, smallest, top_value):
    def one(position, parts):
        draws = jax.random.uniform(jax.random.fold_in(jax.random.fold_in(rng, 6), position), (parts,), jnp.float32, smallest / len(pieces), top_value / len(pieces))
        return jnp.repeat(jnp.exp(draws), dims[position] // parts).reshape((-1,) + (1,) * (len(dims) - position - 1))

    level = one(*pieces[0])
    for cut in pieces[1:]:
        level = level * one(*cut)
    return level


def gaussian(rng, shape, deviation, limit, cuts=(), kind=jnp.bfloat16):
    loudness = shard_levels(rng, shape, cuts, -0.22, 0.18) if cuts else 1.0
    entries = jax.random.normal(rng, shape, jnp.float32) * deviation * loudness
    return jnp.minimum(jnp.maximum(entries, -limit), limit).astype(kind)


def setup_inputs(seed: int = 0) -> dict:
    key_of = jax.random.split(jax.random.key(seed), 7)
    return {
        "factor_blocks": gaussian(key_of[0], (LEVELS - 1, SLOTS, B, B), (8 * B) ** -0.5, 0.125, ((1, 256),)),
        "block_column": place_ends(jax.random.randint(key_of[1], (LEVELS - 1, SLOTS), 0, GRID_ROWS), jax.random.fold_in(key_of[1], 1), 0, GRID_ROWS - 1).astype(jnp.int32),
        "block_row": draw_block_row(jax.random.fold_in(key_of[6], 71), 0),
        "block_count": draw_block_count(jax.random.fold_in(key_of[6], 71), 0),
        "diag_inverse": draw_diag_inverse(jax.random.fold_in(key_of[6], 71), 0),
        "right_side": gaussian(key_of[5], (LEVELS, NODES, R, B), 1.0, 6.0, ((1, 256),), jnp.float32),
    }


def rounded(values):
    return lax.optimization_barrier(values.astype(jnp.bfloat16)).astype(jnp.float32)


def reference(factor_blocks, block_column, block_row, block_count, diag_inverse, right_side):
    slot_ids = jnp.arange(SLOTS, dtype=jnp.int32)
    owner = slot_ids // BLK
    owner_row = owner // GRID_COLS
    owner_col = owner % GRID_COLS
    pending = jnp.zeros((LEVELS * NODES, R, B), jnp.float32)
    forward = []
    for height in range(LEVELS):
        target = right_side[height] - pending[height * NODES:(height + 1) * NODES]
        solved = jnp.einsum("jrb,jab->jra", rounded(target), diag_inverse[height].astype(jnp.float32))
        forward.append(solved)
        if height + 1 < LEVELS:
            column_global = block_column[height] * GRID_COLS + owner_col
            picked = rounded(solved)[column_global]
            update = jnp.einsum("srb,sab->sra", picked, factor_blocks[height].astype(jnp.float32))
            alive_mask = (slot_ids % BLK < block_count[height][owner]).astype(jnp.float32)
            target_row = block_row[height]
            row_global = (target_row // GRID_COLS) * NODES + owner_row * GRID_COLS + target_row % GRID_COLS
            pending = pending.at[row_global].add(update * alive_mask[:, None, None])
    rows_done = jnp.zeros((LEVELS * NODES, R, B), jnp.float32)
    result = [None] * LEVELS
    for height in range(LEVELS - 1, -1, -1):
        target = forward[height]
        if height + 1 < LEVELS:
            target_row = block_row[height]
            row_global = (target_row // GRID_COLS) * NODES + owner_row * GRID_COLS + target_row % GRID_COLS
            column_global = block_column[height] * GRID_COLS + owner_col
            alive_mask = (slot_ids % BLK < block_count[height][owner]).astype(jnp.float32)
            picked = rows_done[row_global]
            contrib = jnp.einsum("sra,sab->srb", picked, factor_blocks[height].astype(jnp.float32))
            summed = jnp.zeros((NODES, R, B), jnp.float32).at[column_global].add(contrib * alive_mask[:, None, None])
            target = target - summed
        solved = jnp.einsum("jra,jab->jrb", rounded(target), diag_inverse[height].astype(jnp.float32))
        result[height] = solved
        rows_done = rows_done.at[height * NODES:(height + 1) * NODES].set(rounded(solved))
    return jnp.stack(forward), jnp.stack(result)
```

```python
import functools

import jax
import jax.numpy as jnp
from jax import lax
from jax.experimental import pallas as pl
from jax.experimental.pallas import tpu as pltpu
from jax.sharding import PartitionSpec as P

MESH = pl.DeviceIdType.MESH
CORES = 2
CHAINS = 4
TABLES = 6


def far_first(ny, nx):
    dist = lambda d, n: min(d, n - d)
    offsets = [(dy, dx) for dy in range(ny) for dx in range(nx)]
    return sorted(offsets, key=lambda o: -(dist(o[0], ny) + dist(o[1], nx)))


def ring_far_first(n):
    return sorted(range(n), key=lambda d: -min(d, n - d))


def solve_kernel(
    dims,
    factor_hbm, diag_hbm, rhs_hbm, column_ref, row_ref, count_ref,
    forward_hbm, result_hbm,
    factor, diag, rhs, y_all, x_all, rhs_first, y_first,
    gathered, picks, terms, sums, row_out, row_in, y_out,
    x_in, x_known, col_terms, col_out, col_in, x_out,
    table_own, table_land, table,
    load_sem, share_sem_s, share_sem_r, table_sem, out_sem, first_sem,
    ag_s, ag_r, rs_s, rs_r, xg_s, xg_r, cs_s, cs_r,
):
    levels, slots, nz, ny, nx, rows, order = dims
    ncol, nrow = ny * nx, CORES * nz
    half = rows // CORES
    width = half // CHAINS
    none = (levels - 1) * slots
    prow, q = lax.axis_index("prow"), lax.axis_index("pcol")
    z, core = lax.div(prow, CORES), lax.rem(prow, CORES)
    y, x = lax.div(q, nx), lax.rem(q, nx)
    other = 1 - core
    sibling = (CORES * z + other, q)
    z_far, xy_far = ring_far_first(nz), far_first(ny, nx)

    def z_partner(dz):
        return lax.rem(z + dz, nz)

    def q_partner(dy, dx):
        return lax.rem(y + dy, ny) * nx + lax.rem(x + dx, nx)

    def remote(src, dst, send, recv, device):
        pltpu.make_async_remote_copy(
            src_ref=src, dst_ref=dst, send_sem=send, recv_sem=recv, device_id=device, device_id_type=MESH
        ).start()

    def wait_for(ref, sem):
        pltpu.make_async_copy(ref, ref, sem).wait()

    def my_half(ref):
        return ref.at[:, 0, pl.ds(pl.multiple_of(core * half, half), half)]

    def other_half(ref):
        return ref.at[:, 0, pl.ds(pl.multiple_of(other * half, half), half)]

    def factor_id(level):
        return level

    def diag_id(level):
        return levels - 1 + level

    rhs_id = 2 * levels - 1

    def load_factor(level):
        i = factor_id(level)
        remote(factor_hbm.at[level], factor.at[core, level], share_sem_s.at[i], share_sem_r.at[i], sibling)
        pltpu.make_async_copy(factor_hbm.at[level], factor.at[core, level], load_sem.at[i]).start()

    def fetch_diag(level):
        pltpu.make_async_copy(diag_hbm.at[level, 0], diag.at[core, level], load_sem.at[diag_id(level)]).start()

    def share_diag(level):
        i = diag_id(level)
        remote(diag_hbm.at[level, 0], diag.at[core, level], share_sem_s.at[i], share_sem_r.at[i], sibling)

    def wait_factor(level):
        i = factor_id(level)
        wait_for(factor.at[core, level], load_sem.at[i])
        wait_for(factor.at[other, level], share_sem_r.at[i])

    def wait_diag(level):
        i = diag_id(level)
        wait_for(diag.at[core, level], load_sem.at[i])
        wait_for(diag.at[other, level], share_sem_r.at[i])

    def send_solved(level, k, found):
        y_out[k, level] = jnp.concatenate(found, axis=0).astype(jnp.bfloat16)
        for dz in z_far:
            remote(
                y_out.at[k, level], gathered.at[k, level, z],
                ag_s.at[k, level], ag_r.at[k, level], (CORES * z_partner(dz) + other, q),
            )

    barrier = pltpu.get_barrier_semaphore()
    partners = [(CORES * z_partner(dz) + other, q) for dz in z_far]
    partners += [(CORES * z + other, q_partner(*o)) for o in xy_far if o != (0, 0)]
    for device in partners:
        pl.semaphore_signal(barrier, inc=1, device_id=device, device_id_type=MESH)

    rhs_copy = pltpu.make_async_copy(rhs_hbm.at[0, 0], rhs_first, first_sem.at[0])
    rhs_copy.start()
    fetch_diag(0)
    pltpu.make_async_copy(my_half(rhs_hbm), rhs.at[core], load_sem.at[rhs_id]).start()
    zero = jnp.zeros((width, order), jnp.float32)
    for k in range(CHAINS):
        for par in range(CORES):
            sums[k, par, none] = zero
    for par in range(CORES):
        col_terms[par, slots] = zero
    rhs_copy.wait()
    wait_for(diag.at[core, 0], load_sem.at[diag_id(0)])
    solved_first = lax.dot_general(
        rhs_first[...].astype(jnp.bfloat16), diag[core, 0], (((1,), (1,)), ((), ())),
        preferred_element_type=jnp.float32,
    )
    y_first[...] = solved_first
    y_all[core, 0] = y_first[pl.ds(pl.multiple_of(core * half, half), half), :]
    index_tables(table_own, column_ref, row_ref, count_ref, levels, slots, ncol, nrow)
    pltpu.make_async_copy(table_own, table.at[core], table_sem.at[0]).start()
    pl.semaphore_wait(barrier, len(partners))

    remote(
        y_first.at[pl.ds(pl.multiple_of(other * half, half), half)], y_all.at[core, 0],
        first_sem.at[1], first_sem.at[2], sibling,
    )
    remote(table_own, table_land, table_sem.at[1], table_sem.at[2], sibling)
    wait_for(y_all.at[other, 0], first_sem.at[2])
    for k in range(CHAINS):
        found = [y_all[par, 0, pl.ds(k * width, width), :] for par in range(CORES)]
        send_solved(0, k, found)
    load_factor(0)
    remote(other_half(rhs_hbm), rhs.at[core], share_sem_s.at[rhs_id], share_sem_r.at[rhs_id], sibling)
    fetch_diag(1)
    share_diag(1)
    share_diag(0)

    def solve_forward(level, k, last):
        chain = pl.ds(k * width, width)
        wait_for(row_in.at[k, level - 1], rs_r.at[k, level - 1])
        total = row_in[k, level - 1, 0].astype(jnp.float32)
        for j in range(1, ncol):
            total += row_in[k, level - 1, j].astype(jnp.float32)
        found = []
        for par in range(CORES):
            target = rhs[par, level, chain, :] - total[par * width : (par + 1) * width]
            solved = lax.dot_general(
                target.astype(jnp.bfloat16), diag[par, level], (((1,), (1,)), ((), ())),
                preferred_element_type=jnp.float32,
            )
            y_all[par, level, chain, :] = solved
            found.append(solved)
        if not last:
            send_solved(level, k, found)

    def update_rows(level, k):
        wait_for(gathered.at[k, level], ag_r.at[k, level])
        for j in range(nz):
            arrived = gathered[k, level, j].astype(jnp.float32)
            for par in range(CORES):
                picks[CORES * j + par] = arrived[par * width : (par + 1) * width]
        for par in range(CORES):
            for s in range(slots):
                picked = picks[table[par, 0, s, level]]
                terms[par, s] = lax.dot_general(
                    picked.astype(jnp.bfloat16), factor[par, level, s], (((1,), (1,)), ((), ())),
                    preferred_element_type=jnp.float32,
                )
        for par in range(CORES):
            for s in range(slots):
                before = table[par, 2, s, level]
                sums[k, par, level * slots + s] = terms[par, s] + sums[k, par, before]
        for o in xy_far:
            r = q_partner(*o)
            both = [sums[k, par, table[par, 4, 0, (level + 1) * ncol + r]] for par in range(CORES)]
            row_out[k, level, r] = jnp.concatenate(both, axis=0).astype(jnp.bfloat16)
            remote(
                row_out.at[k, level, r], row_in.at[k, level, q],
                rs_s.at[k, level], rs_r.at[k, level], (CORES * z + other, r),
            )

    def solve_back(level, k, first, last):
        chain = pl.ds(k * width, width)
        if not first:
            wait_for(col_in.at[k, level], cs_r.at[k, level])
            total = col_in[k, level, 0].astype(jnp.float32)
            for j in range(1, nz):
                total += col_in[k, level, j].astype(jnp.float32)
        found = []
        for par in range(CORES):
            target = y_all[par, level, chain, :]
            if not first:
                target = target - total[par * width : (par + 1) * width]
            solved = jnp.dot(target.astype(jnp.bfloat16), diag[par, level], preferred_element_type=jnp.float32)
            x_all[par, level, chain, :] = solved
            found.append(solved)
        if not last:
            x_out[k, level - 1] = jnp.concatenate(found, axis=0).astype(jnp.bfloat16)
            for o in xy_far:
                r = q_partner(*o)
                remote(
                    x_out.at[k, level - 1], x_in.at[k, level - 1, q],
                    xg_s.at[k, level - 1], xg_r.at[k, level - 1], (CORES * z + other, r),
                )

    def update_columns(level, k):
        wait_for(x_in.at[k, level], xg_r.at[k, level])
        for j in range(ncol):
            arrived = x_in[k, level, j].astype(jnp.float32)
            for par in range(CORES):
                x_known[k, (level + 1) * ncol + j, par] = arrived[par * width : (par + 1) * width]
        for par in range(CORES):
            for s in range(slots):
                picked = x_known[k, table[par, 1, s, level], par]
                terms[par, s] = jnp.dot(picked.astype(jnp.bfloat16), factor[par, level, s], preferred_element_type=jnp.float32)
        for par in range(CORES):
            for s in range(slots):
                col_terms[par, s] = terms[par, s] + col_terms[par, table[par, 3, s, level]]
        for dz in z_far:
            j = z_partner(dz)
            both = []
            for par in range(CORES):
                total = col_terms[0, table[0, 5, 0, level * nrow + CORES * j + par]]
                for part in range(1, CORES):
                    total += col_terms[part, table[part, 5, 0, level * nrow + CORES * j + par]]
                both.append(total)
            col_out[k, level, j] = jnp.concatenate(both, axis=0).astype(jnp.bfloat16)
            remote(
                col_out.at[k, level, j], col_in.at[k, level, z],
                cs_s.at[k, level], cs_r.at[k, level], (CORES * j + other, q),
            )

    wait_for(table_land, table_sem.at[2])
    pltpu.make_async_copy(table_land, table.at[other], table_sem.at[3]).start()
    wait_for(table.at[core], table_sem.at[0])
    wait_for(table.at[other], table_sem.at[3])

    def forward_step(level, first, last):
        if not last:
            load_factor(level + 1)
            fetch_diag(level + 2)
            share_diag(level + 2)
        wait_factor(level)
        for k in range(CHAINS):
            update_rows(level, k)
        if first:
            wait_for(rhs.at[core], load_sem.at[rhs_id])
            wait_for(rhs.at[other], share_sem_r.at[rhs_id])
        wait_diag(level + 1)
        for k in range(CHAINS):
            solve_forward(level + 1, k, last)

    def forward_loop(level, carry):
        forward_step(level, False, False)
        return carry

    forward_step(0, True, False)
    lax.fori_loop(1, levels - 2, forward_loop, 0)
    forward_step(levels - 2, False, True)

    def give(src, out, level, sems):
        here = pl.ds(pl.multiple_of(core * half, half), half)
        pltpu.make_async_copy(src.at[core, level], out.at[level, 0, here], sems.at[0]).start()
        remote(src.at[other, level], out.at[level, 0, here], sems.at[1], sems.at[2], sibling)

    for k in range(CHAINS):
        solve_back(levels - 1, k, True, False)
    give(x_all, result_hbm, levels - 1, out_sem.at[1])
    wait_for(diag.at[other, 0], share_sem_r.at[diag_id(0)])

    def give_forward(level, carry):
        give(y_all, forward_hbm, level, out_sem.at[0])
        return carry

    lax.fori_loop(0, levels, give_forward, 0)

    def back_loop(i, carry):
        level = levels - 2 - i
        for k in range(CHAINS):
            update_columns(level, k)
        for k in range(CHAINS):
            solve_back(level, k, False, False)
        give(x_all, result_hbm, level, out_sem.at[1])
        return carry

    lax.fori_loop(0, levels - 2, back_loop, 0)
    for k in range(CHAINS):
        update_columns(0, k)
    for k in range(CHAINS):
        solve_back(0, k, False, True)
    give(x_all, result_hbm, 0, out_sem.at[1])

    def drain(level, carry):
        for k in range(CHAINS):
            wait_for(gathered.at[k, level], ag_s.at[k, level])
            wait_for(row_out.at[k, level], rs_s.at[k, level])
            wait_for(x_in.at[k, level], xg_s.at[k, level])
            wait_for(col_out.at[k, level], cs_s.at[k, level])
        wait_for(factor.at[core, level], share_sem_s.at[factor_id(level)])
        wait_for(diag.at[core, level], share_sem_s.at[diag_id(level)])
        return carry

    lax.fori_loop(0, levels - 1, drain, 0)
    wait_for(diag.at[core, levels - 1], share_sem_s.at[diag_id(levels - 1)])
    wait_for(rhs.at[core], share_sem_s.at[rhs_id])
    wait_for(table_own, table_sem.at[1])
    wait_for(y_all.at[core, 0], first_sem.at[1])
    for kind, (src, out) in enumerate(((y_all, forward_hbm), (x_all, result_hbm))):
        wait_for(src.at[core], out_sem.at[kind, 0])
        wait_for(src.at[other], out_sem.at[kind, 1])
        wait_for(other_half(out), out_sem.at[kind, 2])


def index_tables(out, column_ref, row_ref, count_ref, levels, slots, ncol, nrow):
    steps = levels - 1
    total = steps * slots
    shape = (8, 128)
    sub = lax.broadcasted_iota(jnp.int32, shape, 0)
    lane = lax.broadcasted_iota(jnp.int32, shape, 1)
    nothing = jnp.full(shape, -1, jnp.int32)
    zeros = jnp.zeros(shape, jnp.int32)
    row_of, column_of = [], []
    row_lanes, column_lanes = nothing, nothing
    rows, columns = zeros, zeros
    for level in range(steps):
        row_keys, column_keys = nothing, nothing
        row_plain, column_plain = zeros, zeros
        count = count_ref[level]
        for s in range(slots):
            row, column = row_ref[level, s], column_ref[level, s]
            live = s < count
            row_key = jnp.where(live, row, -1)
            column_key = jnp.where(live, level * nrow + column, -1)
            row_keys = jnp.where(sub == s, row_key, row_keys)
            column_keys = jnp.where(sub == s, column_key, column_keys)
            row_plain = jnp.where(sub == s, row, row_plain)
            column_plain = jnp.where(sub == s, column, column_plain)
            row_lanes = jnp.where(lane == level * slots + s, row_key, row_lanes)
            column_lanes = jnp.where(lane == level * slots + s, column_key, column_lanes)
        row_of.append(row_keys)
        column_of.append(column_keys)
        rows = jnp.where(lane == level, row_plain, rows)
        columns = jnp.where(lane == level, column_plain, columns)
    before_row, before_column = zeros, zeros
    last_row, last_column = nothing, nothing
    for level in range(steps):
        at = level * slots + sub
        earlier = lane < at
        found = jnp.max(jnp.where((row_of[level] == row_lanes) & earlier, lane, -1), axis=1, keepdims=True)
        before_row = jnp.where(lane == level, jnp.where(found < 0, total, found), before_row)
        found = jnp.max(jnp.where((column_of[level] == column_lanes) & earlier, lane, -1), axis=1, keepdims=True)
        found = jnp.where(found < level * slots, slots, found - level * slots)
        before_column = jnp.where(lane == level, found, before_column)
        valid = sub < slots
        last_row = jnp.maximum(last_row, jnp.where((row_of[level] == lane) & valid, at, -1))
        last_column = jnp.maximum(last_column, jnp.where((column_of[level] == lane) & valid, sub, -1))
    last_row = jnp.max(last_row, axis=0, keepdims=True)
    last_column = jnp.max(last_column, axis=0, keepdims=True)
    out[0] = columns
    out[1] = rows
    out[2] = before_row
    out[3] = before_column
    out[4] = jnp.broadcast_to(jnp.where(last_row < 0, total, last_row), shape)
    out[5] = jnp.broadcast_to(jnp.where(last_column < 0, slots, last_column), shape)


def deliver_kernel(forward_ref, result_ref, forward_out, result_out, stage, read_sem, write_sem):
    reads, writes = [], []
    for kind, (src, dst) in enumerate(((forward_ref, forward_out), (result_ref, result_out))):
        for level in range(src.shape[0]):
            reads.append(pltpu.make_async_copy(src.at[level], stage.at[kind, level], read_sem.at[kind, level]))
            writes.append(pltpu.make_async_copy(stage.at[kind, level], dst.at[level], write_sem.at[kind, level]))
    for read in reads:
        read.start()
    for read, write in zip(reads, writes):
        read.wait()
        write.start()
    for write in writes:
        write.wait()


def per_device(ny, nx, factor_blocks, block_column, block_row, block_count, diag_inverse, right_side):
    nrow, ncol = lax.axis_size("prow"), lax.axis_size("pcol")
    nz = nrow // CORES
    levels, _, rows, order = right_side.shape
    slots = factor_blocks.shape[1]
    half = rows // CORES
    width = half // CHAINS
    steps = levels - 1
    bf16, f32 = jnp.bfloat16, jnp.float32
    dims = (levels, slots, nz, ny, nx, rows, order)
    block, pair = (width, order), (CORES * width, order)
    dma = pltpu.SemaphoreType.DMA
    anywhere = pl.BlockSpec(memory_space=pl.ANY)
    forward, result = pl.pallas_call(
        functools.partial(solve_kernel, dims),
        name="band_solve",
        out_shape=[jax.ShapeDtypeStruct(right_side.shape, f32)] * 2,
        in_specs=[anywhere] * 3 + [pl.BlockSpec(memory_space=pltpu.SMEM)] * 3,
        out_specs=[anywhere] * 2,
        scratch_shapes=[
            pltpu.VMEM((CORES, steps, slots, order, order), bf16),
            pltpu.VMEM((CORES, levels, order, order), bf16),
            pltpu.VMEM((CORES, levels, half, order), f32),
            pltpu.VMEM((CORES, levels, half, order), f32),
            pltpu.VMEM((CORES, levels, half, order), f32),
            pltpu.VMEM((rows, order), f32),
            pltpu.VMEM((rows, order), f32),
            pltpu.VMEM((CHAINS, steps, nz) + pair, bf16),
            pltpu.VMEM((nrow,) + block, f32),
            pltpu.VMEM((CORES, slots) + block, f32),
            pltpu.VMEM((CHAINS, CORES, steps * slots + 1) + block, f32),
            pltpu.VMEM((CHAINS, steps, ncol) + pair, bf16),
            pltpu.VMEM((CHAINS, steps, ncol) + pair, bf16),
            pltpu.VMEM((CHAINS, steps) + pair, bf16),
            pltpu.VMEM((CHAINS, steps, ncol) + pair, bf16),
            pltpu.VMEM((CHAINS, levels * ncol, CORES) + block, f32),
            pltpu.VMEM((CORES, slots + 1) + block, f32),
            pltpu.VMEM((CHAINS, steps, nz) + pair, bf16),
            pltpu.VMEM((CHAINS, steps, nz) + pair, bf16),
            pltpu.VMEM((CHAINS, steps) + pair, bf16),
            pltpu.VMEM((TABLES, 8, 128), jnp.int32),
            pltpu.VMEM((TABLES, 8, 128), jnp.int32),
            pltpu.SMEM((CORES, TABLES, 8, 128), jnp.int32),
            dma((2 * levels,)),
            dma((2 * levels,)),
            dma((2 * levels,)),
            dma((4,)),
            dma((2, 3)),
            dma((3,)),
        ]
        + [dma((CHAINS, steps))] * 8,
        compiler_params=pltpu.CompilerParams(
            collective_id=0, has_side_effects=True, vmem_limit_bytes=56 * 2**20
        ),
        cost_estimate=pl.CostEstimate(
            flops=4 * rows * order * order * slots * levels, bytes_accessed=20 * 2**20, transcendentals=0
        ),
    )(factor_blocks, diag_inverse, right_side, block_column, block_row, block_count.reshape(-1))
    return pl.pallas_call(
        deliver_kernel,
        name="deliver",
        out_shape=[jax.ShapeDtypeStruct(right_side.shape, f32)] * 2,
        in_specs=[anywhere] * 2,
        out_specs=[anywhere] * 2,
        scratch_shapes=[pltpu.VMEM((2,) + right_side.shape, f32), dma((2, levels)), dma((2, levels))],
        cost_estimate=pl.CostEstimate(flops=0, bytes_accessed=2 * 2**20, transcendentals=0),
    )(forward, result)


def solution(mesh):
    ncol = mesh.shape["pcol"]
    nx = 4 if ncol % 4 == 0 else ncol
    return jax.shard_map(
        functools.partial(per_device, ncol // nx, nx),
        mesh=mesh,
        in_specs=(
            P(None, ("prow", "pcol"), None, None),
            P(None, ("prow", "pcol")),
            P(None, ("prow", "pcol")),
            P(None, ("prow", "pcol")),
            P(None, ("prow", "pcol"), None, None),
            P(None, ("prow", "pcol"), None, None),
        ),
        out_specs=(P(None, ("prow", "pcol"), None, None), P(None, ("prow", "pcol"), None, None)),
        check_vma=False,
    )
```

```python
import functools

import jax
import jax.numpy as jnp
from jax import lax
from jax.experimental import pallas as pl
from jax.experimental.pallas import tpu as pltpu
from jax.sharding import PartitionSpec as P

MESH = pl.DeviceIdType.MESH
CORES = 2
CHAINS = 4
TABLES = 6


def far_first(ny, nx):
    dist = lambda d, n: min(d, n - d)
    offsets = [(dy, dx) for dy in range(ny) for dx in range(nx)]
    return sorted(offsets, key=lambda o: -(dist(o[0], ny) + dist(o[1], nx)))


def ring_far_first(n):
    return sorted(range(n), key=lambda d: -min(d, n - d))


def solve_kernel(
    dims,
    factor_hbm, diag_hbm, rhs_hbm, column_hbm, row_hbm, count_hbm,
    forward_hbm, result_hbm,
    factor, diag, rhs, y_all, x_all, rhs_first, y_first, column_ref, row_ref, count_ref,
    gathered, picks, terms, sums, row_out, row_in, y_out,
    x_in, x_known, col_terms, col_out, col_in, x_out,
    table_own, table_land, table,
    load_sem, share_sem_s, share_sem_r, table_sem, out_sem, first_sem, index_sem,
    ag_s, ag_r, rs_s, rs_r, xg_s, xg_r, cs_s, cs_r,
):
    levels, slots, nz, ny, nx, rows, order = dims
    ncol, nrow = ny * nx, CORES * nz
    half = rows // CORES
    width = half // CHAINS
    none = (levels - 1) * slots
    prow, q = lax.axis_index("prow"), lax.axis_index("pcol")
    z, core = lax.div(prow, CORES), lax.rem(prow, CORES)
    y, x = lax.div(q, nx), lax.rem(q, nx)
    other = 1 - core
    sibling = (CORES * z + other, q)
    z_far, xy_far = ring_far_first(nz), far_first(ny, nx)

    z_ids = [lax.rem(z + dz, nz) for dz in z_far]
    q_ids = [lax.rem(y + dy, ny) * nx + lax.rem(x + dx, nx) for dy, dx in xy_far]

    def remote(src, dst, send, recv, device):
        pltpu.make_async_remote_copy(
            src_ref=src, dst_ref=dst, send_sem=send, recv_sem=recv, device_id=device, device_id_type=MESH
        ).start()

    def wait_for(ref, sem):
        pltpu.make_async_copy(ref, ref, sem).wait()

    def my_half(ref):
        return ref.at[:, 0, pl.ds(pl.multiple_of(core * half, half), half)]

    def other_half(ref):
        return ref.at[:, 0, pl.ds(pl.multiple_of(other * half, half), half)]

    def factor_id(level):
        return level

    def diag_id(level):
        return levels - 1 + level

    rhs_id = 2 * levels - 1

    def load_factor(level):
        i = factor_id(level)
        remote(factor_hbm.at[level], factor.at[core, level], share_sem_s.at[i], share_sem_r.at[i], sibling)
        pltpu.make_async_copy(factor_hbm.at[level], factor.at[core, level], load_sem.at[i]).start()

    def fetch_diag(level):
        pltpu.make_async_copy(diag_hbm.at[level, 0], diag.at[core, level], load_sem.at[diag_id(level)]).start()

    def share_diag(level):
        i = diag_id(level)
        remote(diag_hbm.at[level, 0], diag.at[core, level], share_sem_s.at[i], share_sem_r.at[i], sibling)

    def wait_factor(level):
        i = factor_id(level)
        wait_for(factor.at[core, level], load_sem.at[i])
        wait_for(factor.at[other, level], share_sem_r.at[i])

    def wait_diag(level):
        i = diag_id(level)
        wait_for(diag.at[core, level], load_sem.at[i])
        wait_for(diag.at[other, level], share_sem_r.at[i])

    def send_solved(level, k, found):
        y_out[k, level] = jnp.concatenate(found, axis=0).astype(jnp.bfloat16)
        for j in z_ids:
            remote(
                y_out.at[k, level], gathered.at[k, level, z],
                ag_s.at[k, level], ag_r.at[k, level], (CORES * j + other, q),
            )

    barrier = pltpu.get_barrier_semaphore()
    partners = [(CORES * j + other, q) for j in z_ids]
    partners += [(CORES * z + other, r) for r, o in zip(q_ids, xy_far) if o != (0, 0)]
    for device in partners:
        pl.semaphore_signal(barrier, inc=1, device_id=device, device_id_type=MESH)

    rhs_copy = pltpu.make_async_copy(rhs_hbm.at[0, 0], rhs_first, first_sem.at[0])
    rhs_copy.start()
    index_copies = [
        pltpu.make_async_copy(src, dst, index_sem.at[i])
        for i, (src, dst) in enumerate(((column_hbm, column_ref), (row_hbm, row_ref), (count_hbm, count_ref)))
    ]
    for copy in index_copies:
        copy.start()
    fetch_diag(0)
    pltpu.make_async_copy(my_half(rhs_hbm), rhs.at[core], load_sem.at[rhs_id]).start()
    zero = jnp.zeros((width, order), jnp.float32)
    for k in range(CHAINS):
        for par in range(CORES):
            sums[k, par, none] = zero
    for par in range(CORES):
        col_terms[par, slots] = zero
    rhs_copy.wait()
    wait_for(diag.at[core, 0], load_sem.at[diag_id(0)])
    solved_first = lax.dot_general(
        rhs_first[...].astype(jnp.bfloat16), diag[core, 0], (((1,), (1,)), ((), ())),
        preferred_element_type=jnp.float32,
    )
    y_first[...] = solved_first
    y_all[core, 0] = y_first[pl.ds(pl.multiple_of(core * half, half), half), :]
    for copy in index_copies:
        copy.wait()
    index_tables(table_own, column_ref, row_ref, count_ref, levels, slots, ncol, nrow)
    pltpu.make_async_copy(table_own, table.at[core], table_sem.at[0]).start()
    pl.semaphore_wait(barrier, len(partners))

    remote(
        y_first.at[pl.ds(pl.multiple_of(other * half, half), half)], y_all.at[core, 0],
        first_sem.at[1], first_sem.at[2], sibling,
    )
    remote(table_own, table_land, table_sem.at[1], table_sem.at[2], sibling)
    wait_for(y_all.at[other, 0], first_sem.at[2])
    for k in range(CHAINS):
        found = [y_all[par, 0, pl.ds(k * width, width), :] for par in range(CORES)]
        send_solved(0, k, found)
    load_factor(0)
    remote(other_half(rhs_hbm), rhs.at[core], share_sem_s.at[rhs_id], share_sem_r.at[rhs_id], sibling)
    fetch_diag(1)
    share_diag(1)
    share_diag(0)

    def solve_forward(level, k, last):
        chain = pl.ds(k * width, width)
        wait_for(row_in.at[k, level - 1], rs_r.at[k, level - 1])
        total = row_in[k, level - 1, 0].astype(jnp.float32)
        for j in range(1, ncol):
            total += row_in[k, level - 1, j].astype(jnp.float32)
        found = []
        for par in range(CORES):
            target = rhs[par, level, chain, :] - total[par * width : (par + 1) * width]
            solved = lax.dot_general(
                target.astype(jnp.bfloat16), diag[par, level], (((1,), (1,)), ((), ())),
                preferred_element_type=jnp.float32,
            )
            y_all[par, level, chain, :] = solved
            found.append(solved)
        if not last:
            send_solved(level, k, found)

    def update_rows(level, k):
        wait_for(gathered.at[k, level], ag_r.at[k, level])
        for j in range(nz):
            arrived = gathered[k, level, j].astype(jnp.float32)
            for par in range(CORES):
                picks[CORES * j + par] = arrived[par * width : (par + 1) * width]
        for par in range(CORES):
            for s in range(slots):
                picked = picks[table[par, 0, s, level]]
                terms[par, s] = lax.dot_general(
                    picked.astype(jnp.bfloat16), factor[par, level, s], (((1,), (1,)), ((), ())),
                    preferred_element_type=jnp.float32,
                )
        for par in range(CORES):
            for s in range(slots):
                before = table[par, 2, s, level]
                sums[k, par, level * slots + s] = terms[par, s] + sums[k, par, before]
        for r in q_ids:
            both = [sums[k, par, table[par, 4, 0, (level + 1) * ncol + r]] for par in range(CORES)]
            row_out[k, level, r] = jnp.concatenate(both, axis=0).astype(jnp.bfloat16)
            remote(
                row_out.at[k, level, r], row_in.at[k, level, q],
                rs_s.at[k, level], rs_r.at[k, level], (CORES * z + other, r),
            )

    def solve_back(level, k, first, last):
        chain = pl.ds(k * width, width)
        if not first:
            wait_for(col_in.at[k, level], cs_r.at[k, level])
            total = col_in[k, level, 0].astype(jnp.float32)
            for j in range(1, nz):
                total += col_in[k, level, j].astype(jnp.float32)
        found = []
        for par in range(CORES):
            target = y_all[par, level, chain, :]
            if not first:
                target = target - total[par * width : (par + 1) * width]
            solved = jnp.dot(target.astype(jnp.bfloat16), diag[par, level], preferred_element_type=jnp.float32)
            x_all[par, level, chain, :] = solved
            found.append(solved)
        if not last:
            x_out[k, level - 1] = jnp.concatenate(found, axis=0).astype(jnp.bfloat16)
            for r in q_ids:
                remote(
                    x_out.at[k, level - 1], x_in.at[k, level - 1, q],
                    xg_s.at[k, level - 1], xg_r.at[k, level - 1], (CORES * z + other, r),
                )

    def update_columns(level, k):
        wait_for(x_in.at[k, level], xg_r.at[k, level])
        for j in range(ncol):
            arrived = x_in[k, level, j].astype(jnp.float32)
            for par in range(CORES):
                x_known[k, (level + 1) * ncol + j, par] = arrived[par * width : (par + 1) * width]
        for par in range(CORES):
            for s in range(slots):
                picked = x_known[k, table[par, 1, s, level], par]
                terms[par, s] = jnp.dot(picked.astype(jnp.bfloat16), factor[par, level, s], preferred_element_type=jnp.float32)
        for par in range(CORES):
            for s in range(slots):
                col_terms[par, s] = terms[par, s] + col_terms[par, table[par, 3, s, level]]
        for j in z_ids:
            both = []
            for par in range(CORES):
                total = col_terms[0, table[0, 5, 0, level * nrow + CORES * j + par]]
                for part in range(1, CORES):
                    total += col_terms[part, table[part, 5, 0, level * nrow + CORES * j + par]]
                both.append(total)
            col_out[k, level, j] = jnp.concatenate(both, axis=0).astype(jnp.bfloat16)
            remote(
                col_out.at[k, level, j], col_in.at[k, level, z],
                cs_s.at[k, level], cs_r.at[k, level], (CORES * j + other, q),
            )

    wait_for(table_land, table_sem.at[2])
    pltpu.make_async_copy(table_land, table.at[other], table_sem.at[3]).start()
    wait_for(table.at[core], table_sem.at[0])
    wait_for(table.at[other], table_sem.at[3])

    def forward_step(level, first, last):
        if not last:
            load_factor(level + 1)
            fetch_diag(level + 2)
            share_diag(level + 2)
        wait_factor(level)
        for k in range(CHAINS):
            update_rows(level, k)
        if first:
            wait_for(rhs.at[core], load_sem.at[rhs_id])
            wait_for(rhs.at[other], share_sem_r.at[rhs_id])
        wait_diag(level + 1)
        for k in range(CHAINS):
            solve_forward(level + 1, k, last)

    def forward_loop(level, carry):
        forward_step(level, False, False)
        return carry

    forward_step(0, True, False)
    lax.fori_loop(1, levels - 2, forward_loop, 0)
    forward_step(levels - 2, False, True)

    def give(src, out, level, sems):
        here = pl.ds(pl.multiple_of(core * half, half), half)
        pltpu.make_async_copy(src.at[core, level], out.at[level, 0, here], sems.at[0]).start()
        remote(src.at[other, level], out.at[level, 0, here], sems.at[1], sems.at[2], sibling)

    for k in range(CHAINS):
        solve_back(levels - 1, k, True, False)
    give(x_all, result_hbm, levels - 1, out_sem.at[1])
    wait_for(diag.at[other, 0], share_sem_r.at[diag_id(0)])

    def give_forward(level, carry):
        give(y_all, forward_hbm, level, out_sem.at[0])
        return carry

    lax.fori_loop(0, levels, give_forward, 0)

    def drain(level):
        for k in range(CHAINS):
            wait_for(gathered.at[k, level], ag_s.at[k, level])
            wait_for(row_out.at[k, level], rs_s.at[k, level])
            wait_for(x_in.at[k, level], xg_s.at[k, level])
            wait_for(col_out.at[k, level], cs_s.at[k, level])
        wait_for(factor.at[core, level], share_sem_s.at[factor_id(level)])
        wait_for(diag.at[core, level], share_sem_s.at[diag_id(level)])

    def back_loop(i, carry):
        level = levels - 2 - i
        for k in range(CHAINS):
            update_columns(level, k)
        for k in range(CHAINS):
            solve_back(level, k, False, False)
        give(x_all, result_hbm, level, out_sem.at[1])
        drain(level)
        return carry

    lax.fori_loop(0, levels - 2, back_loop, 0)
    for k in range(CHAINS):
        update_columns(0, k)
    drain(0)
    wait_for(diag.at[core, levels - 1], share_sem_s.at[diag_id(levels - 1)])
    wait_for(rhs.at[core], share_sem_s.at[rhs_id])
    wait_for(table_own, table_sem.at[1])
    wait_for(y_all.at[core, 0], first_sem.at[1])
    for k in range(CHAINS):
        solve_back(0, k, False, True)
    give(x_all, result_hbm, 0, out_sem.at[1])

    for kind, (src, out) in enumerate(((y_all, forward_hbm), (x_all, result_hbm))):
        wait_for(src.at[core], out_sem.at[kind, 0])
        wait_for(src.at[other], out_sem.at[kind, 1])
        wait_for(other_half(out), out_sem.at[kind, 2])


def index_tables(out, column_ref, row_ref, count_ref, levels, slots, ncol, nrow):
    steps = levels - 1
    total = steps * slots
    shape = (8, 128)
    sub = lax.broadcasted_iota(jnp.int32, shape, 0)
    lane = lax.broadcasted_iota(jnp.int32, shape, 1)
    nothing = jnp.full(shape, -1, jnp.int32)
    zeros = jnp.zeros(shape, jnp.int32)
    row_of, column_of = [], []
    row_lanes, column_lanes = nothing, nothing
    rows, columns = zeros, zeros
    for level in range(steps):
        row_keys, column_keys = nothing, nothing
        row_plain, column_plain = zeros, zeros
        count = count_ref[level]
        for s in range(slots):
            row, column = row_ref[level, s], column_ref[level, s]
            live = s < count
            row_key = jnp.where(live, row, -1)
            column_key = jnp.where(live, level * nrow + column, -1)
            row_keys = jnp.where(sub == s, row_key, row_keys)
            column_keys = jnp.where(sub == s, column_key, column_keys)
            row_plain = jnp.where(sub == s, row, row_plain)
            column_plain = jnp.where(sub == s, column, column_plain)
            row_lanes = jnp.where(lane == level * slots + s, row_key, row_lanes)
            column_lanes = jnp.where(lane == level * slots + s, column_key, column_lanes)
        row_of.append(row_keys)
        column_of.append(column_keys)
        rows = jnp.where(lane == level, row_plain, rows)
        columns = jnp.where(lane == level, column_plain, columns)
    before_row, before_column = zeros, zeros
    last_row, last_column = nothing, nothing
    for level in range(steps):
        at = level * slots + sub
        earlier = lane < at
        found = jnp.max(jnp.where((row_of[level] == row_lanes) & earlier, lane, -1), axis=1, keepdims=True)
        before_row = jnp.where(lane == level, jnp.where(found < 0, total, found), before_row)
        found = jnp.max(jnp.where((column_of[level] == column_lanes) & earlier, lane, -1), axis=1, keepdims=True)
        found = jnp.where(found < level * slots, slots, found - level * slots)
        before_column = jnp.where(lane == level, found, before_column)
        valid = sub < slots
        last_row = jnp.maximum(last_row, jnp.where((row_of[level] == lane) & valid, at, -1))
        last_column = jnp.maximum(last_column, jnp.where((column_of[level] == lane) & valid, sub, -1))
    last_row = jnp.max(last_row, axis=0, keepdims=True)
    last_column = jnp.max(last_column, axis=0, keepdims=True)
    out[0] = columns
    out[1] = rows
    out[2] = before_row
    out[3] = before_column
    out[4] = jnp.broadcast_to(jnp.where(last_row < 0, total, last_row), shape)
    out[5] = jnp.broadcast_to(jnp.where(last_column < 0, slots, last_column), shape)


def deliver_kernel(forward_ref, result_ref, forward_out, result_out, stage, read_sem, write_sem):
    reads, writes = [], []
    for kind, (src, dst) in enumerate(((forward_ref, forward_out), (result_ref, result_out))):
        for level in range(src.shape[0]):
            reads.append(pltpu.make_async_copy(src.at[level], stage.at[kind, level], read_sem.at[kind, level]))
            writes.append(pltpu.make_async_copy(stage.at[kind, level], dst.at[level], write_sem.at[kind, level]))
    for read in reads:
        read.start()
    for read, write in zip(reads, writes):
        read.wait()
        write.start()
    for write in writes:
        write.wait()


def per_device(ny, nx, factor_blocks, block_column, block_row, block_count, diag_inverse, right_side):
    nrow, ncol = lax.axis_size("prow"), lax.axis_size("pcol")
    nz = nrow // CORES
    levels, _, rows, order = right_side.shape
    slots = factor_blocks.shape[1]
    half = rows // CORES
    width = half // CHAINS
    steps = levels - 1
    bf16, f32 = jnp.bfloat16, jnp.float32
    dims = (levels, slots, nz, ny, nx, rows, order)
    block, pair = (width, order), (CORES * width, order)
    dma = pltpu.SemaphoreType.DMA
    anywhere = pl.BlockSpec(memory_space=pl.ANY)
    forward, result = pl.pallas_call(
        functools.partial(solve_kernel, dims),
        name="band_solve",
        out_shape=[jax.ShapeDtypeStruct(right_side.shape, f32)] * 2,
        in_specs=[anywhere] * 3 + [anywhere] * 3,
        out_specs=[anywhere] * 2,
        scratch_shapes=[
            pltpu.VMEM((CORES, steps, slots, order, order), bf16),
            pltpu.VMEM((CORES, levels, order, order), bf16),
            pltpu.VMEM((CORES, levels, half, order), f32),
            pltpu.VMEM((CORES, levels, half, order), f32),
            pltpu.VMEM((CORES, levels, half, order), f32),
            pltpu.VMEM((rows, order), f32),
            pltpu.VMEM((rows, order), f32),
            pltpu.SMEM(block_column.shape, jnp.int32),
            pltpu.SMEM(block_row.shape, jnp.int32),
            pltpu.SMEM((steps,), jnp.int32),
            pltpu.VMEM((CHAINS, steps, nz) + pair, bf16),
            pltpu.VMEM((nrow,) + block, f32),
            pltpu.VMEM((CORES, slots) + block, f32),
            pltpu.VMEM((CHAINS, CORES, steps * slots + 1) + block, f32),
            pltpu.VMEM((CHAINS, steps, ncol) + pair, bf16),
            pltpu.VMEM((CHAINS, steps, ncol) + pair, bf16),
            pltpu.VMEM((CHAINS, steps) + pair, bf16),
            pltpu.VMEM((CHAINS, steps, ncol) + pair, bf16),
            pltpu.VMEM((CHAINS, levels * ncol, CORES) + block, f32),
            pltpu.VMEM((CORES, slots + 1) + block, f32),
            pltpu.VMEM((CHAINS, steps, nz) + pair, bf16),
            pltpu.VMEM((CHAINS, steps, nz) + pair, bf16),
            pltpu.VMEM((CHAINS, steps) + pair, bf16),
            pltpu.VMEM((TABLES, 8, 128), jnp.int32),
            pltpu.VMEM((TABLES, 8, 128), jnp.int32),
            pltpu.SMEM((CORES, TABLES, 8, 128), jnp.int32),
            dma((2 * levels,)),
            dma((2 * levels,)),
            dma((2 * levels,)),
            dma((4,)),
            dma((2, 3)),
            dma((3,)),
            dma((3,)),
        ]
        + [dma((CHAINS, steps))] * 8,
        compiler_params=pltpu.CompilerParams(
            collective_id=0, has_side_effects=True, vmem_limit_bytes=56 * 2**20
        ),
        cost_estimate=pl.CostEstimate(
            flops=4 * rows * order * order * slots * levels, bytes_accessed=20 * 2**20, transcendentals=0
        ),
    )(factor_blocks, diag_inverse, right_side, block_column, block_row, block_count.reshape(-1))
    return pl.pallas_call(
        deliver_kernel,
        name="deliver",
        out_shape=[jax.ShapeDtypeStruct(right_side.shape, f32)] * 2,
        in_specs=[anywhere] * 2,
        out_specs=[anywhere] * 2,
        scratch_shapes=[pltpu.VMEM((2,) + right_side.shape, f32), dma((2, levels)), dma((2, levels))],
        cost_estimate=pl.CostEstimate(flops=0, bytes_accessed=2 * 2**20, transcendentals=0),
    )(forward, result)


def solution(mesh):
    ncol = mesh.shape["pcol"]
    nx = 4 if ncol % 4 == 0 else ncol
    return jax.shard_map(
        functools.partial(per_device, ncol // nx, nx),
        mesh=mesh,
        in_specs=(
            P(None, ("prow", "pcol"), None, None),
            P(None, ("prow", "pcol")),
            P(None, ("prow", "pcol")),
            P(None, ("prow", "pcol")),
            P(None, ("prow", "pcol"), None, None),
            P(None, ("prow", "pcol"), None, None),
        ),
        out_specs=(P(None, ("prow", "pcol"), None, None), P(None, ("prow", "pcol"), None, None)),
        check_vma=False,
    )
```
